32 devices in a mesh: section: 8 (over z, x), lane: 4 (over y, core).
Axes of the slice: x: 2, y: 2, z: 4, core: 2. Of those that a mesh axis runs over, the one named last changes fastest.
Arguments:
- value_weight: float32 [8, 1024, 256], P('section', 'lane'), may hold values from -0.1875 to 0.1875
- out_weight: float32 [8, 2048, 1024], P('section', 'lane'), may hold values from -0.125 to 0.125
- value_moment: float32 [8, 1024, 256], P('section', 'lane'), may hold values from -6 to 6
- out_moment: float32 [8, 2048, 1024], P('section', 'lane'), may hold values from -6 to 6
- inputs_saved: bfloat16 [2, 2, 8, 512, 1024], P(None, None, 'section', 'lane'), may hold values from -6 to 6
- queries_saved: bfloat16 [2, 2, 8, 512, 2048], P(None, None, 'section', 'lane'), may hold values from -100 to 100
- keys_saved: bfloat16 [2, 2, 8, 512, 256], P(None, None, 'section', 'lane'), may hold values from -5 to 5
- grad_now: bfloat16 [2, 8, 512, 1024], P(None, 'section', 'lane'), may hold values from -6 to 6
- grad_new: bfloat16 [2, 512, 1024], P(None, 'lane'), may hold values from -6 to 6
- bound_now: int32 [2, 8, 4], P(None, None, 'lane'), may hold values from 1 to 127
- bound_new: int32 [2, 4], P(None, 'lane'), may hold values from 1 to 127
Outputs:
- grad_inputs: bfloat16 [2, 2, 8, 512, 1024], P(None, None, 'section', 'lane')
- grad_queries: bfloat16 [2, 2, 8, 512, 2048], P(None, None, 'section', 'lane')
- grad_keys: bfloat16 [2, 2, 8, 512, 256], P(None, None, 'section', 'lane')
- value_weight_new: float32 [8, 1024, 256], P('section', 'lane')
- out_weight_new: float32 [8, 2048, 1024], P('section', 'lane')
- value_moment_new: float32 [8, 1024, 256], P('section', 'lane')
- out_moment_new: float32 [8, 2048, 1024], P('section', 'lane')
The draws below stay inside these ranges and needn't reach their ends.
All inputs are finite; a program needn't handle non-finite values.
Results may differ from the reference program's by a relative error of at most 0.018.
Values may be sent and summed in bfloat16 or wider, within the bound.
No kernel may reach another device: no remote copies, remote signals or barrier semaphores. Data moves between devices by JAX's collectives and lax.ppermute only.
A program may use at most 128 MiB of HBM per device.

```python
import math
import jax
import jax.numpy as jnp
from jax import lax

D = 1024
QUERY_HEAD_COUNT = 16
KEY_VALUE_HEADS = 2
HEAD_SIZE = 128
TOK = 128
MICRO_TICKS = 2
QW = 2048
KVW = 256
RELAY_SECTIONS = 8
LANES = 4
N_LANE = 4


def paired_draw(key):
    base = jax.random.fold_in(key, 7)
    first_random_key, second_random_key = jax.random.split(base, 2)
    query_group = QUERY_HEAD_COUNT // KEY_VALUE_HEADS
    token_rows = LANES * TOK
    key_rows = jnp.clip(jax.random.normal(first_random_key, (2, MICRO_TICKS, RELAY_SECTIONS, token_rows, KEY_VALUE_HEADS, HEAD_SIZE), jnp.float32), -4.0, 4.0)
    query_rows = jnp.clip(jax.random.normal(second_random_key, (2, MICRO_TICKS, RELAY_SECTIONS, token_rows, KEY_VALUE_HEADS, query_group, HEAD_SIZE), jnp.float32), -4.0, 4.0)
    return (query_rows.reshape(2, MICRO_TICKS, RELAY_SECTIONS, token_rows, QW), key_rows.reshape(2, MICRO_TICKS, RELAY_SECTIONS, token_rows, KVW))


def draw_queries_saved(key, part):
    return paired_draw(key)[0].astype(jnp.bfloat16)


def draw_keys_saved(key, part):
    return paired_draw(key)[1].astype(jnp.bfloat16)


def set_ends(values, rng, smallest, high):
    longest = values.shape.index(max(values.shape))
    spots = []
    for shift in (0, 1):
        where = [jax.random.randint(jax.random.fold_in(rng, axis), (), 0, length) for axis, length in enumerate(values.shape)]
        where[longest] = (where[longest] + shift) % values.shape[longest]
        spots.append(tuple(where))
    return values.at[spots[0]].set(smallest).at[spots[1]].set(high)


def level_of(rng, dims, cuts, least, high):
    gain, own = 1.0, jax.random.fold_in(rng, 6)
    for dim, shards_of in cuts:
        draws = jnp.exp(jax.random.uniform(jax.random.fold_in(own, dim), (shards_of,), jnp.float32, least / len(cuts), high / len(cuts)))
        gain = gain * jnp.repeat(draws, dims[dim] // shards_of).reshape([-1 if axis == dim else 1 for axis in range(len(dims))])
    return gain


def bell_draw(rng, extent, scale, reach, cuts=(), dtype=jnp.bfloat16):
    result = scale * jax.random.normal(rng, extent, jnp.float32)
    if cuts:
        result = result * level_of(rng, extent, cuts, -0.22, 0.18)
    return jnp.clip(result, -reach, reach).astype(dtype)


def setup_inputs(seed: int = 0) -> dict:
    splits = jax.random.split(jax.random.key(seed), 12)
    return {
        "value_weight": bell_draw(splits[0], (RELAY_SECTIONS, D, KVW), D ** -0.5, 0.1875, ((0, 8), (1, 4)), jnp.float32),
        "out_weight": bell_draw(splits[1], (RELAY_SECTIONS, QW, D), QW ** -0.5, 0.125, ((0, 8), (1, 4)), jnp.float32),
        "value_moment": bell_draw(splits[2], (RELAY_SECTIONS, D, KVW), 1.0, 6.0, ((0, 8), (1, 4)), jnp.float32),
        "out_moment": bell_draw(splits[3], (RELAY_SECTIONS, QW, D), 1.0, 6.0, ((0, 8), (1, 4)), jnp.float32),
        "inputs_saved": bell_draw(splits[4], (2, MICRO_TICKS, RELAY_SECTIONS, LANES * TOK, D), 1.0, 6.0, ((2, 8), (3, 4))),
        "queries_saved": draw_queries_saved(jax.random.fold_in(splits[11], 71), 0),
        "keys_saved": draw_keys_saved(jax.random.fold_in(splits[11], 71), 0),
        "grad_now": bell_draw(splits[7], (2, RELAY_SECTIONS, LANES * TOK, D), 1.0, 6.0, ((1, 8), (2, 4))),
        "grad_new": bell_draw(splits[8], (2, LANES * TOK, D), 1.0, 6.0, ((1, 4),)),
        "bound_now": set_ends(jax.random.randint(splits[9], (2, RELAY_SECTIONS, LANES), 1, TOK), jax.random.fold_in(splits[9], 1), 1, TOK - 1).astype(jnp.int32),
        "bound_new": set_ends(jax.random.randint(splits[10], (2, LANES), 1, TOK), jax.random.fold_in(splits[10], 1), 1, TOK - 1).astype(jnp.int32),
    }


decay_rate = 0.9
learn_rate = 0.01

def lowered(array):
    return lax.optimization_barrier(array.astype(jnp.bfloat16)).astype(jnp.float32)

def attend(inputs, query_rows, key_rows, cotangent, bounds, w_value, w_out, full):
    relay_lanes, token_rows, _ = inputs.shape
    query_group = QUERY_HEAD_COUNT // KEY_VALUE_HEADS
    scale_factor = 1.0 / math.sqrt(HEAD_SIZE)
    value_matrix = jnp.einsum('ltd,dc->ltc', inputs.astype(jnp.float32), w_value.astype(jnp.float32)).astype(jnp.bfloat16)
    heads_of_query = query_rows.astype(jnp.float32).reshape(relay_lanes, token_rows, KEY_VALUE_HEADS, query_group, HEAD_SIZE)
    heads_of_key = key_rows.astype(jnp.float32).reshape(relay_lanes, token_rows, KEY_VALUE_HEADS, HEAD_SIZE)
    heads_of_value = value_matrix.astype(jnp.float32).reshape(relay_lanes, token_rows, KEY_VALUE_HEADS, HEAD_SIZE)
    scores = jnp.einsum('lihgd,ljhd->lhgij', heads_of_query, heads_of_key) * scale_factor
    places = jnp.arange(token_rows)
    earlier = places[None, :] <= places[:, None]
    second = places[None, :] >= bounds[:, None]
    same_doc = second[:, :, None] == second[:, None, :]
    allowed = (earlier[None] & same_doc)[:, None, None]
    scores = jnp.where(allowed, scores, -1e+30)
    top_score = lax.optimization_barrier(jnp.max(scores, axis=-1, keepdims=True))
    expo = jnp.exp(scores - top_score)
    probs = expo / lax.optimization_barrier(jnp.sum(expo, axis=-1, keepdims=True))
    probs_low = lowered(probs)
    attended = jnp.einsum('lhgij,ljhd->lihgd', probs_low, heads_of_value).astype(jnp.bfloat16).reshape(relay_lanes, token_rows, QW)
    attended_gradient = jnp.einsum('ltd,cd->ltc', cotangent.astype(jnp.float32), w_out.astype(jnp.float32)).astype(jnp.bfloat16)
    head_gradient = attended_gradient.astype(jnp.float32).reshape(relay_lanes, token_rows, KEY_VALUE_HEADS, query_group, HEAD_SIZE)
    grad_values = jnp.einsum('lhgij,lihgd->ljhd', probs_low, head_gradient).astype(jnp.bfloat16).reshape(relay_lanes, token_rows, KVW)
    grad_inputs = (cotangent.astype(jnp.float32) + jnp.einsum('ltc,dc->ltd', grad_values.astype(jnp.float32), w_value.astype(jnp.float32))).astype(jnp.bfloat16)
    if not full:
        return grad_inputs
    grad_probs = jnp.einsum('lihgd,ljhd->lhgij', head_gradient, heads_of_value)
    delta = lax.optimization_barrier(jnp.sum(probs * grad_probs, axis=-1, keepdims=True))
    grad_scores = lowered(probs * (grad_probs - delta) * scale_factor)
    grad_queries = jnp.einsum('lhgij,ljhd->lihgd', grad_scores, heads_of_key).astype(jnp.bfloat16).reshape(relay_lanes, token_rows, QW)
    grad_keys = jnp.einsum('lhgij,lihgd->ljhd', grad_scores, heads_of_query).astype(jnp.bfloat16).reshape(relay_lanes, token_rows, KVW)
    grad_wvalue = jnp.einsum('ltd,ltc->ldc', inputs.astype(jnp.float32), grad_values.astype(jnp.float32))
    grad_wout = jnp.einsum('ltc,ltd->lcd', attended.astype(jnp.float32), cotangent.astype(jnp.float32))
    return (grad_inputs, grad_queries, grad_keys, grad_wvalue, grad_wout)

def reference(value_weight, out_weight, value_moment, out_moment, inputs_saved, queries_saved, keys_saved, grad_now, grad_new, bound_now, bound_new):
    sections = value_weight.shape[0]
    relay_lanes = N_LANE
    value_low = value_weight.astype(jnp.bfloat16)
    out_low = out_weight.astype(jnp.bfloat16)

    def split_rows(array):
        return array.reshape(array.shape[:-2] + (relay_lanes, TOK, array.shape[-1]))
    inputs_all = split_rows(inputs_saved)
    queries_all = split_rows(queries_saved)
    keys_all = split_rows(keys_saved)
    grads_first = split_rows(grad_now)
    grads_fresh = split_rows(grad_new)
    indices = jnp.arange(sections)
    handed = []
    for direction in range(2):

        def tick_zero(place, direction=direction):
            section = place if direction == 0 else sections - 1 - place
            return attend(inputs_all[direction, 0, place], queries_all[direction, 0, place], keys_all[direction, 0, place], grads_first[direction, place], bound_now[direction, place], value_low[section], out_low[section], False)
        handed.append(lax.map(tick_zero, indices))
    second_grads = [jnp.concatenate([handed[0][1:], grads_fresh[0][None]], axis=0), jnp.concatenate([grads_fresh[1][None], handed[1][:-1]], axis=0)]
    second_bounds = [jnp.concatenate([bound_now[0, 1:], bound_new[0][None]], axis=0), jnp.concatenate([bound_new[1][None], bound_now[1, :-1]], axis=0)]
    results = []
    for direction in range(2):

        def both_ticks(place, direction=direction):
            section = place if direction == 0 else sections - 1 - place
            first = attend(inputs_all[direction, 0, place], queries_all[direction, 0, place], keys_all[direction, 0, place], grads_first[direction, place], bound_now[direction, place], value_low[section], out_low[section], True)
            later = attend(inputs_all[direction, 1, place], queries_all[direction, 1, place], keys_all[direction, 1, place], second_grads[direction][place], second_bounds[direction][place], value_low[section], out_low[section], True)
            part_value = lax.optimization_barrier(jnp.sum(lowered(first[3] + later[3]), axis=0))
            part_out = lax.optimization_barrier(jnp.sum(lowered(first[4] + later[4]), axis=0))
            return ((first[0], later[0]), (first[1], later[1]), (first[2], later[2]), part_value, part_out)
        results.append(lax.map(both_ticks, indices))

    def assemble(slot, width):
        stacked = jnp.stack([jnp.stack([results[r][slot][0], results[r][slot][1]]) for r in range(2)])
        return stacked.reshape(2, MICRO_TICKS, sections, relay_lanes * TOK, width)
    grad_inputs = assemble(0, D)
    grad_queries = assemble(1, QW)
    grad_keys = assemble(2, KVW)
    grad_value = (results[0][3] + results[1][3][::-1]) / relay_lanes
    grad_out = (results[0][4] + results[1][4][::-1]) / relay_lanes
    value_moment_new = decay_rate * value_moment + grad_value
    out_moment_new = decay_rate * out_moment + grad_out
    value_weight_new = value_weight - learn_rate * value_moment_new
    out_weight_new = out_weight - learn_rate * out_moment_new
    return (grad_inputs, grad_queries, grad_keys, value_weight_new, out_weight_new, value_moment_new, out_moment_new)
```

```python
import functools
import math

import jax
import jax.numpy as jnp
from jax import lax
from jax.experimental import pallas as pl
from jax.experimental.pallas import tpu as pltpu
from jax.sharding import PartitionSpec as P

HEAD = 128
KV_HEADS = 2

decay_rate = 0.9
learn_rate = 0.01

BF = jnp.bfloat16
F32 = jnp.float32
SCALE = 1.0 / math.sqrt(HEAD)


def mm(a, b, ca, cb):
    return lax.dot_general(a, b, (((ca,), (cb,)), ((), ())), preferred_element_type=F32)


def after(x, *others):
    return lax.optimization_barrier((x, *others))[0]


def piece(array, *lead):
    rest = array.shape[len(lead) :]
    return array, pl.BlockSpec((None,) * len(lead) + rest, lambda i, *s: lead + (0,) * len(rest))


def whole_out(shape):
    return pl.BlockSpec(shape, lambda i, *s: (0,) * len(shape))


def call(kernel, name, scalars, operands, shapes, flops, size, steps=1, outs=None, scratch=(), aliases=None):
    arrays, specs = zip(*operands)
    grid = pltpu.PrefetchScalarGridSpec(
        num_scalar_prefetch=len(scalars),
        grid=(steps,),
        in_specs=list(specs),
        out_specs=outs or [whole_out(s.shape) for s in shapes],
        scratch_shapes=scratch,
    )
    aliases = {len(scalars) + i: o for i, o in (aliases or {}).items()}
    return pl.pallas_call(
        kernel,
        grid_spec=grid,
        out_shape=shapes,
        input_output_aliases=aliases,
        compiler_params=pltpu.CompilerParams(vmem_limit_bytes=20 * 1024 * 1024),
        cost_estimate=pl.CostEstimate(flops=1, bytes_accessed=1, transcendentals=0),
        name=name,
    )(*scalars, *arrays)


def sds(shape, dtype=BF):
    return jax.ShapeDtypeStruct(shape, dtype)


def head_start(meta, i, per):
    place = jnp.bitwise_xor(meta[1], i // per) * per + i % per
    return place * HEAD


def columns(ref, start, size):
    return ref[:, pl.ds(pl.multiple_of(start, HEAD), size)]


def value_kernel(lanes, meta, x, *refs):
    parts, (full, out) = refs[:lanes], refs[lanes:]
    rows = parts[0].shape[1]
    for r in range(2):
        for k in range(lanes):
            at = jnp.bitwise_xor(meta[3], k) * rows
            full[r, pl.ds(pl.multiple_of(at, rows), rows), :] = parts[k][r]
        for t in range(x.shape[1]):
            out[r, t] = mm(x[r, t, 0], full[r], 1, 0).astype(BF)


def values_of(meta, inputs, parts):
    ticks, tok, d = inputs.shape[1], inputs.shape[3], inputs.shape[4]
    kvw = parts[0].shape[2]
    return call(
        functools.partial(value_kernel, len(parts)),
        "values",
        [meta],
        [piece(inputs)] + [piece(p) for p in parts],
        [sds((2, d, kvw)), sds((2, ticks, tok, kvw))],
        4 * ticks * tok * d * kvw,
        4 << 20,
    )


def queries_of(half, heads, per, meta, q):
    base = half * heads * HEAD
    return jnp.concatenate([columns(q, base + head_start(meta, i, per), HEAD) for i in range(heads)], axis=0)


def front_kernel(r, per, heads, sections, meta, bounds, q, k, v, probs, mine, send):
    t = pl.program_id(0)
    tok = q.shape[0]
    place = meta[2]
    near = jnp.clip(place + t * (1 - 2 * r), 0, sections - 1)
    at = jnp.where((t == 1) & (meta[4 + r] == 1), 2 * sections + r, r * sections + near)
    bound = bounds[at]
    key_at = lax.broadcasted_iota(jnp.int32, (tok, tok), 0)
    query_at = lax.broadcasted_iota(jnp.int32, (tok, tok), 1)
    seen = (key_at <= query_at) & ((query_at >= bound) == (key_at >= bound))
    seen = jnp.concatenate([seen.astype(F32)] * heads, axis=1) > 0.5
    for s in range(2):
        half = meta[0] if s == 0 else 1 - meta[0]
        out = mine if s == 0 else send
        key, val = columns(k, half * HEAD, HEAD), columns(v, half * HEAD, HEAD)
        x = jnp.where(seen, mm(key, queries_of(half, heads, per, meta, q), 1, 1) * SCALE, -1e30)
        e = jnp.exp(x - jnp.max(x, axis=0, keepdims=True))
        p = (e * (1.0 / jnp.sum(e, axis=0, keepdims=True))).astype(BF)
        probs[s] = p
        for i in range(heads):
            out[:, i * HEAD : (i + 1) * HEAD] = mm(p[:, i * tok : (i + 1) * tok], val, 0, 0).astype(BF)


def front(r, per, heads, sections, meta, bounds, queries, keys, values):
    ticks, tok = queries.shape[1], queries.shape[3]
    width = heads * HEAD
    operands = [
        (queries, pl.BlockSpec((None, None, None, tok, 2 * width), lambda t, *s: (r, t, 0, 0, 0))),
        (keys, pl.BlockSpec((None, None, None, tok, 2 * HEAD), lambda t, *s: (r, t, 0, 0, 0))),
        (values, pl.BlockSpec((None, None, tok, 2 * HEAD), lambda t, *s: (r, t, 0, 0))),
    ]
    outs = [
        pl.BlockSpec((None, 2, tok, heads * tok), lambda t, *s: (t, 0, 0, 0)),
        pl.BlockSpec((None, tok, width), lambda t, *s: (t, 0, 0)),
        pl.BlockSpec((None, tok, width), lambda t, *s: (t, 0, 0)),
    ]
    shapes = [sds((ticks, 2, tok, heads * tok)), sds((ticks, tok, width)), sds((ticks, tok, width))]
    return call(
        functools.partial(front_kernel, r, per, heads, sections),
        "front",
        [meta, bounds],
        operands,
        shapes,
        2 * ticks * 2 * heads * 2 * tok * tok * HEAD * 4,
        8 << 20,
        ticks,
        outs,
    )


def chosen(meta, r, refs):
    return refs[0][...] if len(refs) == 1 else jnp.where(meta[4 + r] == 1, refs[1][...], refs[0][...])


def ahead_kernel(r, t, parts, per, meta, *refs):
    own, par, weights = refs[: t + 1], refs[t + 1 : 2 * t + 2], refs[2 * t + 2 : -2]
    tok = own[0].shape[0]
    g = jnp.concatenate([chosen(meta, r, own), chosen(meta, r, par)], axis=0)
    for k in range(parts):
        ga = mm(g, weights[k][...], 1, 1).astype(BF)
        for j in range(per):
            for s in range(2):
                at = (k * per + j) * tok
                refs[s - 2][at : at + tok, :] = ga[s * tok : (s + 1) * tok, j * HEAD : (j + 1) * HEAD]


def ahead(r, t, per, meta, own, par, weights):
    tok, d = own[0][0].shape[-2:]
    shape = (len(weights) * per * tok, HEAD)
    return call(
        functools.partial(ahead_kernel, r, t, len(weights), per),
        "ahead",
        [meta],
        own + par + [piece(w) for w in weights],
        [sds(shape)] * 2,
        4 * d * shape[0] * HEAD * 2,
        4 << 20,
    )


def middle_kernel(r, t, meta, *refs):
    own = refs[: t + 1]
    probs, mine, came, w, gv_out, gi_out = refs[t + 1 :]
    h = meta[0] == 0
    a = mm(probs[0], mine[...], 1, 0).astype(BF)
    b = mm(probs[1], came[...], 1, 0).astype(BF)
    gv = jnp.concatenate([jnp.where(h, a, b), jnp.where(h, b, a)], axis=1)
    gv_out[...] = gv
    gi_out[...] = (chosen(meta, r, own).astype(F32) + mm(gv, w[...], 1, 1)).astype(BF)


def middle(r, t, meta, own, probs, mine, came, w_value):
    tok, d = own[0][0].shape[-2:]
    return call(
        functools.partial(middle_kernel, r, t),
        "middle",
        [meta],
        own + [piece(probs, t), piece(mine), piece(came), piece(w_value, r)],
        [sds((tok, 2 * HEAD)), sds((tok, d))],
        4 * tok * d * 2 * HEAD,
        2 << 20,
    )


def back_kernel(per, heads, filled, meta, q, k, v, probs, mine0, came0, mine1, came1, *refs):
    gq, gk = refs[2:] if filled else refs
    tok = q.shape[2]
    width = heads * HEAD
    for t, pair in enumerate(((mine0, came0), (mine1, came1))):
        for s in range(2):
            half = meta[0] if s == 0 else 1 - meta[0]
            base = half * width
            key, val = columns(k.at[t, 0], half * HEAD, HEAD), columns(v.at[t], half * HEAD, HEAD)
            gp = mm(val, pair[s][...], 1, 1)
            p = probs[t, s].astype(F32)
            delta = jnp.sum(p * gp, axis=0, keepdims=True)
            gs = (p * ((gp - delta) * SCALE)).astype(BF)
            for i in range(heads):
                at = pl.multiple_of(base + head_start(meta, i, per), HEAD)
                out = mm(gs[:, i * tok : (i + 1) * tok], key, 0, 0).astype(BF)
                gq.at[t, 0][:, pl.ds(at, HEAD)] = out
            out = mm(gs, queries_of(half, heads, per, meta, q.at[t, 0]), 1, 0).astype(BF)
            gk.at[t, 0][:, pl.ds(pl.multiple_of(half * HEAD, HEAD), HEAD)] = out


def back(r, per, heads, meta, queries, keys, values, probs, gas, filled=()):
    arrays = (queries, keys)
    specs = [pl.BlockSpec((None,) + a.shape[1:], lambda i, m: (r, 0, 0, 0, 0)) for a in arrays]
    operands = list(zip(arrays, specs)) + [piece(values, r), piece(probs)] + [piece(a) for a in gas]
    operands += [(a, pl.BlockSpec(memory_space=pl.ANY)) for a in filled]
    first = len(operands) - 2
    return call(
        functools.partial(back_kernel, per, heads, bool(filled)),
        "back",
        [meta],
        operands,
        [sds(a.shape) for a in arrays],
        2 * 2 * 2 * heads * 3 * queries.shape[3] ** 2 * HEAD * 4,
        8 << 20,
        outs=specs,
        aliases={first: 0, first + 1: 1} if filled else {},
    )


def outer_kernel(r, meta, mine, came, *refs):
    out = refs[-1]
    total = mm(mine[0], refs[0][...], 0, 0)
    total = total + mm(came[0], refs[1][...], 0, 0)
    total = total + mm(mine[1], chosen(meta, r, refs[2:4]), 0, 0)
    total = total + mm(came[1], chosen(meta, r, refs[4:6]), 0, 0)
    out[...] = total.astype(out.dtype)


def outer(r, k, rows, meta, mine, came, gs, dtype):
    ticks, tok = mine.shape[0], mine.shape[1]
    d = gs[0][0].shape[-1]
    step = min(rows, 256)
    first = k * (rows // step)
    block = pl.BlockSpec((ticks, tok, step), lambda i, m: (0, 0, first + i))
    outs = [pl.BlockSpec((step, d), lambda i, m: (i, 0))]
    return call(
        functools.partial(outer_kernel, r),
        "outer",
        [meta],
        [(mine, block), (came, block)] + gs,
        [sds((rows, d), dtype)],
        4 * ticks * tok * rows * d,
        4 << 20,
        rows // step,
        outs,
    )[0]


def value_grad_kernel(meta, x, gv00, gv01, gv10, gv11, own, *refs):
    sent, total = refs[:-1], refs[-1]
    rows = own.shape[1]
    for r, gvs in enumerate(((gv00, gv01), (gv10, gv11))):
        total[...] = mm(x[r, 0, 0], gvs[0][...], 0, 0) + mm(x[r, 1, 0], gvs[1][...], 0, 0)
        for k, out in enumerate((own, *sent)):
            at = jnp.bitwise_xor(meta[3], k) * rows
            out[r] = total[pl.ds(pl.multiple_of(at, rows), rows), :].astype(out.dtype)


def value_grads(meta, lanes, inputs, gvs):
    d = inputs.shape[4]
    kvw = KV_HEADS * HEAD
    rows = d // lanes
    shapes = [sds((2, rows, kvw), F32)] + [sds((2, rows, kvw))] * (lanes - 1)
    return call(
        value_grad_kernel,
        "value_grads",
        [meta],
        [piece(a) for a in (inputs, *gvs)],
        shapes,
        4 * 2 * inputs.shape[3] * d * kvw,
        4 << 20,
        scratch=[pltpu.VMEM((d, kvw), F32)],
    )


def shards(
    value_weight,
    out_weight,
    value_moment,
    out_moment,
    inputs_saved,
    queries_saved,
    keys_saved,
    grad_now,
    grad_new,
    bound_now,
    bound_new,
):
    sections = lax.axis_size("section")
    lanes = lax.axis_size("lane")
    place = lax.axis_index("section")
    lane = lax.axis_index("lane")
    half = lanes // KV_HEADS
    h, c = lane // half, lane % half
    rows = out_weight.shape[1]
    per = rows // HEAD
    heads = per * half
    at_end = (place == sections - 1, place == 0)
    meta = jnp.stack([h, c, place, lane, *at_end]).astype(jnp.int32)

    def at_lane(x, k):
        return lax.ppermute(x, "lane", [(i, i ^ k) for i in range(lanes)])

    def partner(x):
        return at_lane(x, half)

    def mirrored(x):
        return lax.ppermute(x, "section", [(i, sections - 1 - i) for i in range(sections)])

    def relayed(x, r, k=0):
        by = 1 if r else -1
        pairs = [
            (i * lanes + j, (i + by) * lanes + (j ^ k))
            for i in range(sections)
            for j in range(lanes)
            if 0 <= i + by < sections
        ]
        return lax.ppermute(x, ("section", "lane"), pairs)

    def at_ends(x):
        pairs = [(i * lanes + j, i * lanes + (j ^ half)) for i in (0, sections - 1) for j in range(lanes)]
        return lax.ppermute(x, ("section", "lane"), pairs)

    own_value = value_weight[0].astype(BF)
    mirror_value = mirrored(own_value)
    own_out = [after(out_weight, own_value)[0].astype(BF)]
    mirror_out = [mirrored(after(own_out[0], mirror_value))]

    def with_mates(pieces):
        spread = [[p] + [at_lane(p, k) for k in range(1, half)] for p in pieces]
        return [s[k] for k in range(half) for s in spread]

    parts_out = [with_mates(own_out)]
    g_par = partner(after(grad_now, mirror_value)[:, 0])
    fresh_par = at_ends(lax.dynamic_index_in_dim(grad_new, jnp.where(place == 0, 1, 0), keepdims=False))
    bounds = jnp.concatenate([bound_now.reshape(-1), bound_new.reshape(-1)])

    own, par = {}, {}
    for r in range(2):
        own[r, 0], par[r, 0] = [piece(grad_now, r, 0)], [piece(g_par, r)]
    ga, gv, gi = {}, {}, {}
    probs, mine, came = [None] * 2, [None] * 2, [None] * 2

    def run_ahead(r, t, *deps):
        weights = list(after(tuple(parts_out[r]), *deps)) if deps else parts_out[r]
        here, send = ahead(r, t, per, meta, own[r, t], par[r, t], weights)
        ga[r, t] = (here, partner(send))

    def run_front(r, v):
        probs[r], mine[r], send = front(r, per, heads, sections, meta, bounds, queries_saved, keys_saved, v)
        came[r] = partner(send)

    def run_middle(r, t, *deps):
        p = after(probs[r], *deps) if deps else probs[r]
        gv[r, t], gi[r, t] = middle(r, t, meta, own[r, t], p, *ga[r, t], w_value)

    def run_relay(r, *deps):
        sent = after(gi[r, 0], *deps) if deps else gi[r, 0]
        own[r, 1] = [piece(relayed(sent, r)), piece(grad_new, r)]
        par[r, 1] = [piece(relayed(sent, r, half)), piece(fresh_par)]

    def run_outer(r, *deps):
        m = after(mine[r], *deps) if deps else mine[r]
        gs = own[r, 0] + par[r, 0] + own[r, 1] + par[r, 1]
        away = [outer(r, k, rows, meta, m, came[r], gs, BF) for k in range(1, half)]
        total = outer(r, 0, rows, meta, after(m, *away) if away else m, came[r], gs, F32)
        for k, part in enumerate(away):
            total = total + at_lane(part, k + 1).astype(F32)
        return total

    both_value = jnp.stack([own_value, mirror_value])
    parts_value = [both_value] + [at_lane(both_value, k) for k in range(1, lanes)]
    run_ahead(0, 0)
    w_value, values = values_of(meta, inputs_saved, parts_value)
    run_front(0, values)
    run_middle(0, 0)
    run_front(1, after(values, gi[0, 0]))
    parts_out.append(with_mates(after(tuple(mirror_out), probs[1], came[0], came[1])))
    run_ahead(1, 0)
    run_middle(1, 0)
    run_relay(1)
    run_relay(0, gi[1, 0])
    relays = [own[0, 1][0][0], par[0, 1][0][0]]
    total1 = run_outer(1, *relays)
    cut = rows // 2
    send_out = total1.astype(BF)
    back_first = mirrored(send_out[:cut])
    run_ahead(0, 1, send_out)
    run_ahead(1, 1, ga[0, 1][0])
    total0 = run_outer(0, ga[1, 1][0])
    sums_out = [total0, total1]
    run_middle(0, 1, total0)
    run_middle(1, 1, gi[0, 1])
    back_second = mirrored(after(send_out, back_first, gi[1, 1])[cut:])
    gas = [[*ga[r, 0], *ga[r, 1]] for r in range(2)]
    out = back(0, per, heads, meta, queries_saved, keys_saved, values, after(probs[0], gi[1, 1]), gas[0])
    gvs = [gv[r, t] for r in range(2) for t in range(2)]
    total, *sent = value_grads(meta, lanes, inputs_saved, gvs)
    for k, part in enumerate(sent):
        total = total + at_lane(part, k + 1).astype(F32)
    sums_value = [total[0], total[1]]
    back_value = mirrored(total[1].astype(BF))
    grad_queries, grad_keys = back(
        1, per, heads, meta, queries_saved, keys_saved, values, after(probs[1], sent[0]), gas[1], out
    )
    grad_inputs = jnp.stack([jnp.stack([gi[r, t] for t in range(2)]) for r in range(2)])[:, :, None]
    back_out = jnp.concatenate([back_first, back_second], axis=0)
    back_out = after(back_out, grad_queries)
    mean_value = (sums_value[0] + back_value.astype(F32)) / lanes
    mean_out = (sums_out[0] + back_out.astype(F32)) / lanes
    value_moment_new = decay_rate * value_moment + mean_value[None]
    out_moment_new = decay_rate * out_moment + mean_out[None]
    value_weight_new = value_weight - learn_rate * value_moment_new
    out_weight_new = out_weight - learn_rate * out_moment_new

    return (
        grad_inputs,
        grad_queries,
        grad_keys,
        value_weight_new,
        out_weight_new,
        value_moment_new,
        out_moment_new,
    )


def solution(mesh):
    saved = P(None, None, "section", "lane", None)
    weight = P("section", "lane", None)
    return jax.shard_map(
        shards,
        mesh=mesh,
        in_specs=(
            weight,
            weight,
            weight,
            weight,
            saved,
            saved,
            saved,
            P(None, "section", "lane", None),
            P(None, "lane", None),
            P(None, None, "lane"),
            P(None, "lane"),
        ),
        out_specs=(saved, saved, saved, weight, weight, weight, weight),
        check_vma=False,
    )
```

```python
import functools
import math

import jax
import jax.numpy as jnp
from jax import lax
from jax.experimental import pallas as pl
from jax.experimental.pallas import tpu as pltpu
from jax.sharding import PartitionSpec as P

HEAD = 128
KV_HEADS = 2

decay_rate = 0.9
learn_rate = 0.01

BF = jnp.bfloat16
F32 = jnp.float32
SCALE = 1.0 / math.sqrt(HEAD)


def mm(a, b, ca, cb):
    return lax.dot_general(a, b, (((ca,), (cb,)), ((), ())), preferred_element_type=F32)


def piece(array, *lead):
    rest = array.shape[len(lead) :]
    return array, pl.BlockSpec((None,) * len(lead) + rest, lambda i, *s: lead + (0,) * len(rest))


def whole_out(shape):
    return pl.BlockSpec(shape, lambda i, *s: (0,) * len(shape))


def call(kernel, name, scalars, operands, shapes, steps=1, outs=None, scratch=(), aliases=None, deps=()):
    count = len(scalars) + len(operands)

    def body(*refs):
        kernel(*refs[:count], *refs[count + len(deps) :])

    operands = list(operands) + [(a, pl.BlockSpec(memory_space=pl.ANY)) for a in deps]
    arrays, specs = zip(*operands)
    grid = pltpu.PrefetchScalarGridSpec(
        num_scalar_prefetch=len(scalars),
        grid=(steps,),
        in_specs=list(specs),
        out_specs=outs or [whole_out(s.shape) for s in shapes],
        scratch_shapes=scratch,
    )
    aliases = {len(scalars) + i: o for i, o in (aliases or {}).items()}
    return pl.pallas_call(
        body,
        grid_spec=grid,
        out_shape=shapes,
        input_output_aliases=aliases,
        compiler_params=pltpu.CompilerParams(vmem_limit_bytes=20 * 1024 * 1024),
        cost_estimate=pl.CostEstimate(flops=1, bytes_accessed=1, transcendentals=0),
        name=name,
    )(*scalars, *arrays)


def sds(shape, dtype=BF):
    return jax.ShapeDtypeStruct(shape, dtype)


def head_start(meta, i, per):
    place = jnp.bitwise_xor(meta[1], i // per) * per + i % per
    return place * HEAD


def columns(ref, start, size):
    return ref[:, pl.ds(pl.multiple_of(start, HEAD), size)]


def hold_kernel(x, out):
    pass


def hold(x, deps):
    anywhere = pl.BlockSpec(memory_space=pl.ANY)
    shape = [sds(x.shape, x.dtype)]
    return call(hold_kernel, "hold", [], [(x, anywhere)], shape, outs=[anywhere], aliases={0: 0}, deps=deps)[0]


def cast_kernel(x, out):
    out[...] = x[...].astype(BF)


def lowered(i, rows, x, deps=()):
    d = x.shape[2]
    block = pl.BlockSpec((None, rows, d), lambda _: (0, i, 0))
    return call(cast_kernel, "lowered", [], [(x, block)], [sds((rows, d))], deps=deps)[0]


def value_kernel(lanes, meta, x, *refs):
    parts, (full, out) = refs[:-2], refs[-2:]
    rows = parts[0].shape[0]
    for r in range(2):
        for k in range(lanes):
            at = jnp.bitwise_xor(meta[3], k) * rows
            full[r, pl.ds(pl.multiple_of(at, rows), rows), :] = parts[r * lanes + k][...]
        for t in range(x.shape[1]):
            out[r, t] = mm(x[r, t, 0], full[r], 1, 0).astype(BF)


def values_of(meta, inputs, parts, deps=()):
    ticks, tok, d = inputs.shape[1], inputs.shape[3], inputs.shape[4]
    kvw = parts[0].shape[1]
    return call(
        functools.partial(value_kernel, len(parts) // 2),
        "values",
        [meta],
        [piece(inputs)] + [piece(p) for p in parts],
        [sds((2, d, kvw)), sds((2, ticks, tok, kvw))],
        deps=deps,
    )


def queries_of(half, heads, per, meta, q):
    base = half * heads * HEAD
    return jnp.concatenate([columns(q, base + head_start(meta, i, per), HEAD) for i in range(heads)], axis=0)


def front_kernel(r, per, heads, sections, meta, bounds, q, k, v, probs, mine, send):
    t = pl.program_id(0)
    tok = q.shape[0]
    place = meta[2]
    near = jnp.clip(place + t * (1 - 2 * r), 0, sections - 1)
    at = jnp.where((t == 1) & (meta[4 + r] == 1), 2 * sections + r, r * sections + near)
    bound = bounds[at]
    key_at = lax.broadcasted_iota(jnp.int32, (tok, tok), 0)
    query_at = lax.broadcasted_iota(jnp.int32, (tok, tok), 1)
    seen = (key_at <= query_at) & ((query_at >= bound) == (key_at >= bound))
    seen = jnp.concatenate([seen.astype(F32)] * heads, axis=1) > 0.5
    for s in range(2):
        half = meta[0] if s == 0 else 1 - meta[0]
        out = mine if s == 0 else send
        key, val = columns(k, half * HEAD, HEAD), columns(v, half * HEAD, HEAD)
        x = jnp.where(seen, mm(key, queries_of(half, heads, per, meta, q), 1, 1) * SCALE, -1e30)
        e = jnp.exp(x - jnp.max(x, axis=0, keepdims=True))
        p = (e * (1.0 / jnp.sum(e, axis=0, keepdims=True))).astype(BF)
        probs[s] = p
        for i in range(heads):
            out[:, i * HEAD : (i + 1) * HEAD] = mm(p[:, i * tok : (i + 1) * tok], val, 0, 0).astype(BF)


def front(r, per, heads, sections, meta, bounds, queries, keys, values, deps=()):
    ticks, tok = queries.shape[1], queries.shape[3]
    width = heads * HEAD
    operands = [
        (queries, pl.BlockSpec((None, None, None, tok, 2 * width), lambda t, *s: (r, t, 0, 0, 0))),
        (keys, pl.BlockSpec((None, None, None, tok, 2 * HEAD), lambda t, *s: (r, t, 0, 0, 0))),
        (values, pl.BlockSpec((None, None, tok, 2 * HEAD), lambda t, *s: (r, t, 0, 0))),
    ]
    outs = [
        pl.BlockSpec((None, 2, tok, heads * tok), lambda t, *s: (t, 0, 0, 0)),
        pl.BlockSpec((None, tok, width), lambda t, *s: (t, 0, 0)),
        pl.BlockSpec((None, tok, width), lambda t, *s: (t, 0, 0)),
    ]
    shapes = [sds((ticks, 2, tok, heads * tok)), sds((ticks, tok, width)), sds((ticks, tok, width))]
    return call(
        functools.partial(front_kernel, r, per, heads, sections),
        "front",
        [meta, bounds],
        operands,
        shapes,
        ticks,
        outs,
        deps=deps,
    )


def chosen(meta, r, refs):
    return refs[0][...] if len(refs) == 1 else jnp.where(meta[4 + r] == 1, refs[1][...], refs[0][...])


def ahead_kernel(r, t, parts, per, meta, *refs):
    own, par, weights = refs[: t + 1], refs[t + 1 : 2 * t + 2], refs[2 * t + 2 : -2]
    tok = own[0].shape[0]
    g = jnp.concatenate([chosen(meta, r, own), chosen(meta, r, par)], axis=0)
    for k in range(parts):
        ga = mm(g, weights[k][...], 1, 1).astype(BF)
        for j in range(per):
            for s in range(2):
                at = (k * per + j) * tok
                refs[s - 2][at : at + tok, :] = ga[s * tok : (s + 1) * tok, j * HEAD : (j + 1) * HEAD]


def ahead(r, t, per, meta, own, par, weights, deps=()):
    tok, d = own[0][1].block_shape[-2:]
    shape = (len(weights) * per * tok, HEAD)
    return call(
        functools.partial(ahead_kernel, r, t, len(weights), per),
        "ahead",
        [meta],
        own + par + [piece(w) for w in weights],
        [sds(shape)] * 2,
        deps=deps,
    )


def middle_kernel(r, t, meta, *refs):
    own = refs[: t + 1]
    probs, mine, came, w, gv_out, gi_out, *joined = refs[t + 1 :]
    h = meta[0] == 0
    a = mm(probs[0], mine[...], 1, 0).astype(BF)
    b = mm(probs[1], came[...], 1, 0).astype(BF)
    gv = jnp.concatenate([jnp.where(h, a, b), jnp.where(h, b, a)], axis=1)
    gv_out[...] = gv
    gi = (chosen(meta, r, own).astype(F32) + mm(gv, w[...], 1, 1)).astype(BF)
    gi_out[...] = gi
    if joined:
        joined[0][:, : gi.shape[1]] = gi
        joined[0][:, gi.shape[1] :] = gv


def middle(r, t, meta, own, probs, mine, came, w_value, joined, deps=()):
    tok, d = own[0][1].block_shape[-2:]
    return call(
        functools.partial(middle_kernel, r, t),
        "middle",
        [meta],
        own + [piece(probs, t), piece(mine), piece(came), piece(w_value, r)],
        [sds((tok, 2 * HEAD)), sds((tok, d))] + [sds((tok, d + 2 * HEAD))] * joined,
        deps=deps,
    )


def back_kernel(per, heads, filled, meta, q, k, v, probs, mine0, came0, mine1, came1, *refs):
    gq, gk = refs[2:] if filled else refs
    tok = q.shape[2]
    width = heads * HEAD
    for t, pair in enumerate(((mine0, came0), (mine1, came1))):
        for s in range(2):
            half = meta[0] if s == 0 else 1 - meta[0]
            base = half * width
            key, val = columns(k.at[t, 0], half * HEAD, HEAD), columns(v.at[t], half * HEAD, HEAD)
            gp = mm(val, pair[s][...], 1, 1)
            p = probs[t, s].astype(F32)
            delta = jnp.sum(p * gp, axis=0, keepdims=True)
            gs = (p * ((gp - delta) * SCALE)).astype(BF)
            for i in range(heads):
                at = pl.multiple_of(base + head_start(meta, i, per), HEAD)
                out = mm(gs[:, i * tok : (i + 1) * tok], key, 0, 0).astype(BF)
                gq.at[t, 0][:, pl.ds(at, HEAD)] = out
            out = mm(gs, queries_of(half, heads, per, meta, q.at[t, 0]), 1, 0).astype(BF)
            gk.at[t, 0][:, pl.ds(pl.multiple_of(half * HEAD, HEAD), HEAD)] = out


def back(r, per, heads, meta, queries, keys, values, probs, gas, filled=(), deps=()):
    arrays = (queries, keys)
    specs = [pl.BlockSpec((None,) + a.shape[1:], lambda i, m: (r, 0, 0, 0, 0)) for a in arrays]
    operands = list(zip(arrays, specs)) + [piece(values, r), piece(probs)] + [piece(a) for a in gas]
    operands += [(a, pl.BlockSpec(memory_space=pl.ANY)) for a in filled]
    first = len(operands) - 2
    return call(
        functools.partial(back_kernel, per, heads, bool(filled)),
        "back",
        [meta],
        operands,
        [sds(a.shape) for a in arrays],
        outs=specs,
        aliases={first: 0, first + 1: 1} if filled else {},
        deps=deps,
    )


def outer_kernel(r, meta, mine, came, *refs):
    out = refs[-1]
    total = mm(mine[0], refs[0][...], 0, 0)
    total = total + mm(came[0], refs[1][...], 0, 0)
    total = total + mm(mine[1], chosen(meta, r, refs[2:4]), 0, 0)
    total = total + mm(came[1], chosen(meta, r, refs[4:6]), 0, 0)
    out[...] = total.astype(out.dtype)


def outer(r, k, rows, meta, mine, came, gs, dtype, deps=()):
    ticks, tok = mine.shape[0], mine.shape[1]
    d = gs[0][1].block_shape[-1]
    step = min(rows, 256)
    first = k * (rows // step)
    block = pl.BlockSpec((ticks, tok, step), lambda i, m: (0, 0, first + i))
    outs = [pl.BlockSpec((step, d), lambda i, m: (i, 0))]
    return call(
        functools.partial(outer_kernel, r),
        "outer",
        [meta],
        [(mine, block), (came, block)] + gs,
        [sds((rows, d), dtype)],
        rows // step,
        outs,
        deps=deps,
    )[0]


def update_kernel(lanes, meta, own, back, moment, weight, moment_out, weight_out):
    grad = (own[...] + back[...].astype(F32)) / lanes
    new = decay_rate * moment[...] + grad
    moment_out[...] = new
    weight_out[...] = weight[...] - learn_rate * new


def update(lanes, meta, own, back, moment, weight, deps=()):
    rows, d = own.shape
    step = min(rows, 128)
    flat = pl.BlockSpec((step, d), lambda i, m: (i, 0))
    deep = pl.BlockSpec((None, step, d), lambda i, m: (0, i, 0))
    return call(
        functools.partial(update_kernel, lanes),
        "update",
        [meta],
        [(own, flat), (back, flat), (moment, deep), (weight, deep)],
        [sds(moment.shape, F32)] * 2,
        rows // step,
        [deep, deep],
        deps=deps,
    )


def value_grad_kernel(meta, x, gv00, gv01, gv10, gv11, own, *refs):
    sent, total = refs[:-1], refs[-1]
    rows = own.shape[1]
    for r, gvs in enumerate(((gv00, gv01), (gv10, gv11))):
        total[...] = mm(x[r, 0, 0], gvs[0][...], 0, 0) + mm(x[r, 1, 0], gvs[1][...], 0, 0)
        for k, out in enumerate((own, *sent)):
            at = jnp.bitwise_xor(meta[3], k) * rows
            out[r] = total[pl.ds(pl.multiple_of(at, rows), rows), :].astype(out.dtype)


def value_grads(meta, lanes, inputs, gvs, deps=()):
    d = inputs.shape[4]
    kvw = KV_HEADS * HEAD
    rows = d // lanes
    shapes = [sds((2, rows, kvw), F32)] + [sds((2, rows, kvw))] * (lanes - 1)
    return call(
        value_grad_kernel,
        "value_grads",
        [meta],
        [piece(a) for a in (inputs, *gvs)],
        shapes,
        scratch=[pltpu.VMEM((d, kvw), F32)],
        deps=deps,
    )


def shards(
    value_weight,
    out_weight,
    value_moment,
    out_moment,
    inputs_saved,
    queries_saved,
    keys_saved,
    grad_now,
    grad_new,
    bound_now,
    bound_new,
):
    sections = lax.axis_size("section")
    lanes = lax.axis_size("lane")
    place = lax.axis_index("section")
    lane = lax.axis_index("lane")
    half = lanes // KV_HEADS
    h, c = lane // half, lane % half
    rows = out_weight.shape[1]
    per = rows // HEAD
    heads = per * half
    at_end = (place == sections - 1, place == 0)
    meta = jnp.stack([h, c, place, lane, *at_end]).astype(jnp.int32)

    def at_lane(x, k):
        return lax.ppermute(x, "lane", [(i, i ^ k) for i in range(lanes)])

    def partner(x):
        return at_lane(x, half)

    def mirrored(x):
        return lax.ppermute(x, "section", [(i, sections - 1 - i) for i in range(sections)])

    def relayed(x, r, k=0):
        by = 1 if r else -1
        pairs = [
            (i * lanes + j, (i + by) * lanes + (j ^ k))
            for i in range(sections)
            for j in range(lanes)
            if 0 <= i + by < sections
        ]
        return lax.ppermute(x, ("section", "lane"), pairs)

    def at_ends(x):
        pairs = [(i * lanes + j, i * lanes + (j ^ half)) for i in (0, sections - 1) for j in range(lanes)]
        return lax.ppermute(x, ("section", "lane"), pairs)

    def spread(x, count):
        return [x] + [at_lane(x, k) for k in range(1, count)]

    def summed(away, total):
        for k, part in enumerate(away):
            if part.shape[0] == rows:
                step = part.shape[0] // 4
                pieces = [at_lane(part[i : i + step], k + 1) for i in range(0, part.shape[0], step)]
                part = jnp.concatenate(pieces, axis=0)
            else:
                part = at_lane(part, k + 1)
            total = total + part.astype(F32)
        return total

    own_value = value_weight[0].astype(BF)
    mirror_value = mirrored(own_value)
    own_out = lowered(0, rows, out_weight)
    mirror_out = mirrored(hold(own_out, [mirror_value]))
    parts_value = spread(own_value, lanes) + spread(mirror_value, lanes)
    cut = rows // 4

    def with_mates(x):
        pieces = [x[i : i + cut] for i in range(0, rows, cut)]
        table = [spread(p, half) for p in pieces]
        if cut % HEAD:
            return [jnp.concatenate([row[k] for row in table], axis=0) for k in range(half)]
        return [row[k] for k in range(half) for row in table]

    parts_out = [with_mates(own_out)]
    fresh_par = at_ends(lax.dynamic_index_in_dim(grad_new, jnp.where(place == 0, 1, 0), keepdims=False))
    g_par = partner(grad_now[:, 0])
    bounds = jnp.concatenate([bound_now.reshape(-1), bound_new.reshape(-1)])

    own, par = {}, {}
    ga, gv, gi = {}, {}, {}
    probs, mine, came = [None] * 2, [None] * 2, [None] * 2
    for r in range(2):
        own[r, 0], par[r, 0] = [piece(grad_now, r, 0)], [piece(g_par, r)]

    def run_front(r, deps=()):
        probs[r], mine[r], send = front(
            r, per, heads, sections, meta, bounds, queries_saved, keys_saved, values, deps
        )
        came[r] = jnp.stack([partner(send[t]) for t in range(2)])

    def run_ahead(r, t, deps=()):
        here, send = ahead(r, t, heads // len(parts_out[r]), meta, own[r, t], par[r, t], parts_out[r], deps)
        if (r, t) == (1, 1):
            step = send.shape[0] // 2
            ga[r, t] = (here, jnp.concatenate([partner(send[:step]), partner(send[step:])], axis=0))
        else:
            ga[r, t] = (here, partner(send))

    def run_middle(r, t, deps=()):
        gv[r, t], gi[r, t], *joined = middle(
            r, t, meta, own[r, t], probs[r], *ga[r, t], w_value, 0, deps
        )
        return joined

    def run_relay(r):
        own[r, 1] = [piece(relayed(gi[r, 0], r)), piece(grad_new, r)]
        par[r, 1] = [piece(relayed(gi[r, 0], r, half)), piece(fresh_par)]

    def run_outer(r, deps=()):
        gs = own[r, 0] + par[r, 0] + own[r, 1] + par[r, 1]
        away = [outer(r, k, rows, meta, mine[r], came[r], gs, BF, deps) for k in range(1, half)]
        total = outer(r, 0, rows, meta, mine[r], came[r], gs, F32, [*deps, *away])
        return summed(away, total)

    run_ahead(0, 0)
    w_value, values = values_of(meta, inputs_saved, parts_value, [ga[0, 0][0], fresh_par])
    run_front(0)
    run_front(1, [probs[0]])
    run_middle(0, 0, [probs[1]])
    mirror_out = hold(mirror_out, [came[0], came[1], gi[0, 0]])
    parts_out.append(with_mates(mirror_out))
    run_ahead(1, 0)
    run_middle(1, 0)
    run_relay(1)
    gi[0, 0] = hold(gi[0, 0], [gi[1, 0]])
    run_relay(0)
    relays = [own[0, 1][0][0], par[0, 1][0][0]]
    total1 = run_outer(1, relays)
    send_out = total1.astype(BF)
    back_out = mirrored(send_out)
    run_ahead(1, 1, [send_out])
    run_ahead(0, 1, [ga[1, 1][0]])
    run_middle(1, 1, [ga[0, 1][0]])
    run_middle(0, 1, [gi[1, 1]])
    gvs = [gv[r, t] for r in range(2) for t in range(2)]
    total, *sent = value_grads(meta, lanes, inputs_saved, gvs)
    gas = [[*ga[r, 0], *ga[r, 1]] for r in range(2)]
    total0 = run_outer(0, [total])
    out = back(1, per, heads, meta, queries_saved, keys_saved, values, probs[1], gas[1], deps=[total0])
    total = [summed([part[r] for part in sent], total[r]) for r in range(2)]
    back_value = mirrored(total[1].astype(BF))
    grad_queries, grad_keys = back(
        0, per, heads, meta, queries_saved, keys_saved, values, probs[0], gas[0], out
    )
    grad_inputs = jnp.stack([jnp.stack([gi[r, t] for t in range(2)]) for r in range(2)])[:, :, None]
    out_moment_new, out_weight_new = update(
        lanes, meta, total0, back_out, out_moment, out_weight, [grad_keys]
    )
    mean_value = (total[0] + back_value.astype(F32)) / lanes
    value_moment_new = decay_rate * value_moment + mean_value[None]
    value_weight_new = value_weight - learn_rate * value_moment_new
    return (
        grad_inputs,
        grad_queries,
        grad_keys,
        value_weight_new,
        out_weight_new,
        value_moment_new,
        out_moment_new,
    )


def solution(mesh):
    saved = P(None, None, "section", "lane", None)
    weight = P("section", "lane", None)
    return jax.shard_map(
        shards,
        mesh=mesh,
        in_specs=(
            weight,
            weight,
            weight,
            weight,
            saved,
            saved,
            saved,
            P(None, "section", "lane", None),
            P(None, "lane", None),
            P(None, None, "lane"),
            P(None, "lane"),
        ),
        out_specs=(saved, saved, saved, weight, weight, weight, weight),
        check_vma=False,
    )
```

```python
import functools
import math

import jax
import jax.numpy as jnp
from jax import lax
from jax.experimental import pallas as pl
from jax.experimental.pallas import tpu as pltpu
from jax.sharding import PartitionSpec as P

HEAD = 128
KV_HEADS = 2

decay_rate = 0.9
learn_rate = 0.01

BF = jnp.bfloat16
F32 = jnp.float32
SCALE = 1.0 / math.sqrt(HEAD)


def mm(a, b, ca, cb):
    return lax.dot_general(a, b, (((ca,), (cb,)), ((), ())), preferred_element_type=F32)


def piece(array, *lead):
    rest = array.shape[len(lead) :]
    return array, pl.BlockSpec((None,) * len(lead) + rest, lambda i, *s: lead + (0,) * len(rest))


def whole_out(shape):
    return pl.BlockSpec(shape, lambda i, *s: (0,) * len(shape))


def call(kernel, name, scalars, operands, shapes, steps=1, outs=None, scratch=(), aliases=None, deps=()):
    count = len(scalars) + len(operands)

    def body(*refs):
        kernel(*refs[:count], *refs[count + len(deps) :])

    operands = list(operands) + [(a, pl.BlockSpec(memory_space=pl.ANY)) for a in deps]
    arrays, specs = zip(*operands)
    grid = pltpu.PrefetchScalarGridSpec(
        num_scalar_prefetch=len(scalars),
        grid=(steps,),
        in_specs=list(specs),
        out_specs=outs or [whole_out(s.shape) for s in shapes],
        scratch_shapes=scratch,
    )
    aliases = {len(scalars) + i: o for i, o in (aliases or {}).items()}
    return pl.pallas_call(
        body,
        grid_spec=grid,
        out_shape=shapes,
        input_output_aliases=aliases,
        compiler_params=pltpu.CompilerParams(vmem_limit_bytes=20 * 1024 * 1024),
        cost_estimate=pl.CostEstimate(flops=1, bytes_accessed=1, transcendentals=0),
        name=name,
    )(*scalars, *arrays)


def sds(shape, dtype=BF):
    return jax.ShapeDtypeStruct(shape, dtype)


def head_start(meta, i, per):
    place = jnp.bitwise_xor(meta[1], i // per) * per + i % per
    return place * HEAD


def columns(ref, start, size):
    return ref[:, pl.ds(pl.multiple_of(start, HEAD), size)]


def hold_kernel(x, out):
    pass


def hold(x, deps):
    anywhere = pl.BlockSpec(memory_space=pl.ANY)
    shape = [sds(x.shape, x.dtype)]
    return call(hold_kernel, "hold", [], [(x, anywhere)], shape, outs=[anywhere], aliases={0: 0}, deps=deps)[0]


def cast_kernel(x, out):
    out[...] = x[...].astype(BF)


def lowered(i, rows, x, deps=()):
    d = x.shape[2]
    block = pl.BlockSpec((None, rows, d), lambda _: (0, i, 0))
    return call(cast_kernel, "lowered", [], [(x, block)], [sds((rows, d))], deps=deps)[0]


def value_kernel(lanes, meta, x, *refs):
    parts, (full, out) = refs[:-2], refs[-2:]
    rows = parts[0].shape[0]
    for r in range(2):
        for k in range(lanes):
            at = jnp.bitwise_xor(meta[3], k) * rows
            full[r, pl.ds(pl.multiple_of(at, rows), rows), :] = parts[r * lanes + k][...]
        for t in range(x.shape[1]):
            out[r, t] = mm(x[r, t, 0], full[r], 1, 0).astype(BF)


def values_of(meta, inputs, parts, deps=()):
    ticks, tok, d = inputs.shape[1], inputs.shape[3], inputs.shape[4]
    kvw = parts[0].shape[1]
    return call(
        functools.partial(value_kernel, len(parts) // 2),
        "values",
        [meta],
        [piece(inputs)] + [piece(p) for p in parts],
        [sds((2, d, kvw)), sds((2, ticks, tok, kvw))],
        deps=deps,
    )


def queries_of(half, heads, per, meta, q):
    base = half * heads * HEAD
    return jnp.concatenate([columns(q, base + head_start(meta, i, per), HEAD) for i in range(heads)], axis=0)


def front_kernel(r, per, heads, sections, meta, bounds, q, k, v, probs, mine, send):
    t = pl.program_id(0)
    tok = q.shape[0]
    place = meta[2]
    near = jnp.clip(place + t * (1 - 2 * r), 0, sections - 1)
    at = jnp.where((t == 1) & (meta[4 + r] == 1), 2 * sections + r, r * sections + near)
    bound = bounds[at]
    key_at = lax.broadcasted_iota(jnp.int32, (tok, tok), 0)
    query_at = lax.broadcasted_iota(jnp.int32, (tok, tok), 1)
    seen = (key_at <= query_at) & ((query_at >= bound) == (key_at >= bound))
    seen = jnp.concatenate([seen.astype(F32)] * heads, axis=1) > 0.5
    for s in range(2):
        half = meta[0] if s == 0 else 1 - meta[0]
        out = mine if s == 0 else send
        key, val = columns(k, half * HEAD, HEAD), columns(v, half * HEAD, HEAD)
        x = jnp.where(seen, mm(key, queries_of(half, heads, per, meta, q), 1, 1) * SCALE, -1e30)
        e = jnp.exp(x - jnp.max(x, axis=0, keepdims=True))
        p = (e * (1.0 / jnp.sum(e, axis=0, keepdims=True))).astype(BF)
        probs[s] = p
        for i in range(heads):
            out[:, i * HEAD : (i + 1) * HEAD] = mm(p[:, i * tok : (i + 1) * tok], val, 0, 0).astype(BF)


def front(r, per, heads, sections, meta, bounds, queries, keys, values, deps=()):
    ticks, tok = queries.shape[1], queries.shape[3]
    width = heads * HEAD
    operands = [
        (queries, pl.BlockSpec((None, None, None, tok, 2 * width), lambda t, *s: (r, t, 0, 0, 0))),
        (keys, pl.BlockSpec((None, None, None, tok, 2 * HEAD), lambda t, *s: (r, t, 0, 0, 0))),
        (values, pl.BlockSpec((None, None, tok, 2 * HEAD), lambda t, *s: (r, t, 0, 0))),
    ]
    outs = [
        pl.BlockSpec((None, 2, tok, heads * tok), lambda t, *s: (t, 0, 0, 0)),
        pl.BlockSpec((None, tok, width), lambda t, *s: (t, 0, 0)),
        pl.BlockSpec((None, tok, width), lambda t, *s: (t, 0, 0)),
    ]
    shapes = [sds((ticks, 2, tok, heads * tok)), sds((ticks, tok, width)), sds((ticks, tok, width))]
    return call(
        functools.partial(front_kernel, r, per, heads, sections),
        "front",
        [meta, bounds],
        operands,
        shapes,
        ticks,
        outs,
        deps=deps,
    )


def chosen(meta, r, refs):
    return refs[0][...] if len(refs) == 1 else jnp.where(meta[4 + r] == 1, refs[1][...], refs[0][...])


def ahead_kernel(r, t, parts, per, meta, *refs):
    own, par, weights = refs[: t + 1], refs[t + 1 : 2 * t + 2], refs[2 * t + 2 : -2]
    tok = own[0].shape[0]
    g = jnp.concatenate([chosen(meta, r, own), chosen(meta, r, par)], axis=0)
    for k in range(parts):
        ga = mm(g, weights[k][...], 1, 1).astype(BF)
        for j in range(per):
            for s in range(2):
                at = (k * per + j) * tok
                refs[s - 2][at : at + tok, :] = ga[s * tok : (s + 1) * tok, j * HEAD : (j + 1) * HEAD]


def ahead(r, t, per, meta, own, par, weights, deps=()):
    tok, d = own[0][1].block_shape[-2:]
    shape = (len(weights) * per * tok, HEAD)
    return call(
        functools.partial(ahead_kernel, r, t, len(weights), per),
        "ahead",
        [meta],
        own + par + [piece(w) for w in weights],
        [sds(shape)] * 2,
        deps=deps,
    )


def middle_kernel(r, t, meta, *refs):
    own = refs[: t + 1]
    probs, mine, came, w, gv_out, gi_out, *joined = refs[t + 1 :]
    h = meta[0] == 0
    a = mm(probs[0], mine[...], 1, 0).astype(BF)
    b = mm(probs[1], came[...], 1, 0).astype(BF)
    gv = jnp.concatenate([jnp.where(h, a, b), jnp.where(h, b, a)], axis=1)
    gv_out[...] = gv
    gi = (chosen(meta, r, own).astype(F32) + mm(gv, w[...], 1, 1)).astype(BF)
    gi_out[...] = gi
    if joined:
        joined[0][:, : gi.shape[1]] = gi
        joined[0][:, gi.shape[1] :] = gv


def middle(r, t, meta, own, probs, mine, came, w_value, joined, deps=()):
    tok, d = own[0][1].block_shape[-2:]
    return call(
        functools.partial(middle_kernel, r, t),
        "middle",
        [meta],
        own + [piece(probs, t), piece(mine), piece(came), piece(w_value, r)],
        [sds((tok, 2 * HEAD)), sds((tok, d))] + [sds((tok, d + 2 * HEAD))] * joined,
        deps=deps,
    )


def back_kernel(per, heads, filled, meta, q, k, v, probs, mine0, came0, mine1, came1, *refs):
    gq, gk = refs[2:] if filled else refs
    tok = q.shape[2]
    width = heads * HEAD
    for t, pair in enumerate(((mine0, came0), (mine1, came1))):
        for s in range(2):
            half = meta[0] if s == 0 else 1 - meta[0]
            base = half * width
            key, val = columns(k.at[t, 0], half * HEAD, HEAD), columns(v.at[t], half * HEAD, HEAD)
            gp = mm(val, pair[s][...], 1, 1)
            p = probs[t, s].astype(F32)
            delta = jnp.sum(p * gp, axis=0, keepdims=True)
            gs = (p * ((gp - delta) * SCALE)).astype(BF)
            for i in range(heads):
                at = pl.multiple_of(base + head_start(meta, i, per), HEAD)
                out = mm(gs[:, i * tok : (i + 1) * tok], key, 0, 0).astype(BF)
                gq.at[t, 0][:, pl.ds(at, HEAD)] = out
            out = mm(gs, queries_of(half, heads, per, meta, q.at[t, 0]), 1, 0).astype(BF)
            gk.at[t, 0][:, pl.ds(pl.multiple_of(half * HEAD, HEAD), HEAD)] = out


def back(r, per, heads, meta, queries, keys, values, probs, gas, filled=(), deps=()):
    arrays = (queries, keys)
    specs = [pl.BlockSpec((None,) + a.shape[1:], lambda i, m: (r, 0, 0, 0, 0)) for a in arrays]
    operands = list(zip(arrays, specs)) + [piece(values, r), piece(probs)] + [piece(a) for a in gas]
    operands += [(a, pl.BlockSpec(memory_space=pl.ANY)) for a in filled]
    first = len(operands) - 2
    return call(
        functools.partial(back_kernel, per, heads, bool(filled)),
        "back",
        [meta],
        operands,
        [sds(a.shape) for a in arrays],
        outs=specs,
        aliases={first: 0, first + 1: 1} if filled else {},
        deps=deps,
    )


def outer_kernel(r, meta, mine, came, *refs):
    out = refs[-1]
    total = mm(mine[0], refs[0][...], 0, 0)
    total = total + mm(came[0], refs[1][...], 0, 0)
    total = total + mm(mine[1], chosen(meta, r, refs[2:4]), 0, 0)
    total = total + mm(came[1], chosen(meta, r, refs[4:6]), 0, 0)
    out[...] = total.astype(out.dtype)


def outer(r, k, rows, meta, mine, came, gs, dtype, deps=()):
    ticks, tok = mine.shape[0], mine.shape[1]
    d = gs[0][1].block_shape[-1]
    step = min(rows, 256)
    first = k * (rows // step)
    block = pl.BlockSpec((ticks, tok, step), lambda i, m: (0, 0, first + i))
    outs = [pl.BlockSpec((step, d), lambda i, m: (i, 0))]
    return call(
        functools.partial(outer_kernel, r),
        "outer",
        [meta],
        [(mine, block), (came, block)] + gs,
        [sds((rows, d), dtype)],
        rows // step,
        outs,
        deps=deps,
    )[0]


def update_kernel(lanes, meta, own, back, moment, weight, moment_out, weight_out, done):
    grad = (own[...] + back[...].astype(F32)) / lanes
    new = decay_rate * moment[...] + grad
    moment_out[...] = new
    weight_out[...] = weight[...] - learn_rate * new
    done[...] = new[:8, :HEAD]


def update(lanes, meta, own, back, moment, weight, deps=()):
    rows, d = own.shape
    step = min(rows, 128)
    flat = pl.BlockSpec((step, d), lambda i, m: (i, 0))
    deep = pl.BlockSpec((None, step, d), lambda i, m: (0, i, 0))
    return call(
        functools.partial(update_kernel, lanes),
        "update",
        [meta],
        [(own, flat), (back, flat), (moment, deep), (weight, deep)],
        [sds(moment.shape, F32)] * 2 + [sds((8, HEAD), F32)],
        rows // step,
        [deep, deep, pl.BlockSpec((8, HEAD), lambda i, m: (0, 0))],
        deps=deps,
    )


def value_grad_kernel(meta, x, gv00, gv01, gv10, gv11, own, *refs):
    sent, total = refs[:-1], refs[-1]
    rows = own.shape[1]
    for r, gvs in enumerate(((gv00, gv01), (gv10, gv11))):
        total[...] = mm(x[r, 0, 0], gvs[0][...], 0, 0) + mm(x[r, 1, 0], gvs[1][...], 0, 0)
        for k, out in enumerate((own, *sent)):
            at = jnp.bitwise_xor(meta[3], k) * rows
            out[r] = total[pl.ds(pl.multiple_of(at, rows), rows), :].astype(out.dtype)


def value_grads(meta, lanes, inputs, gvs, deps=()):
    d = inputs.shape[4]
    kvw = KV_HEADS * HEAD
    rows = d // lanes
    shapes = [sds((2, rows, kvw), F32)] + [sds((2, rows, kvw))] * (lanes - 1)
    return call(
        value_grad_kernel,
        "value_grads",
        [meta],
        [piece(a) for a in (inputs, *gvs)],
        shapes,
        scratch=[pltpu.VMEM((d, kvw), F32)],
        deps=deps,
    )


def shards(
    value_weight,
    out_weight,
    value_moment,
    out_moment,
    inputs_saved,
    queries_saved,
    keys_saved,
    grad_now,
    grad_new,
    bound_now,
    bound_new,
):
    sections = lax.axis_size("section")
    lanes = lax.axis_size("lane")
    place = lax.axis_index("section")
    lane = lax.axis_index("lane")
    half = lanes // KV_HEADS
    h, c = lane // half, lane % half
    rows = out_weight.shape[1]
    per = rows // HEAD
    heads = per * half
    at_end = (place == sections - 1, place == 0)
    meta = jnp.stack([h, c, place, lane, *at_end]).astype(jnp.int32)

    def at_lane(x, k):
        return lax.ppermute(x, "lane", [(i, i ^ k) for i in range(lanes)])

    def partner(x):
        return at_lane(x, half)

    def mirrored(x):
        return lax.ppermute(x, "section", [(i, sections - 1 - i) for i in range(sections)])

    def relayed(x, r, k=0):
        by = 1 if r else -1
        pairs = [
            (i * lanes + j, (i + by) * lanes + (j ^ k))
            for i in range(sections)
            for j in range(lanes)
            if 0 <= i + by < sections
        ]
        return lax.ppermute(x, ("section", "lane"), pairs)

    def at_ends(x):
        pairs = [(i * lanes + j, i * lanes + (j ^ half)) for i in (0, sections - 1) for j in range(lanes)]
        return lax.ppermute(x, ("section", "lane"), pairs)

    def spread(x, count):
        return [x] + [at_lane(x, k) for k in range(1, count)]

    def summed(away, total):
        for k, part in enumerate(away):
            if part.shape[0] == rows:
                step = part.shape[0] // 4
                pieces = [at_lane(part[i : i + step], k + 1) for i in range(0, part.shape[0], step)]
                part = jnp.concatenate(pieces, axis=0)
            else:
                part = at_lane(part, k + 1)
            total = total + part.astype(F32)
        return total

    own_value = value_weight[0].astype(BF)
    mirror_value = mirrored(own_value)
    own_out = lowered(0, rows, out_weight)
    mirror_out = mirrored(hold(own_out, [mirror_value]))
    parts_value = spread(own_value, lanes) + spread(mirror_value, lanes)
    cut = rows // 4

    def with_mates(x):
        pieces = [x[i : i + cut] for i in range(0, rows, cut)]
        table = [spread(p, half) for p in pieces]
        if cut % HEAD:
            return [jnp.concatenate([row[k] for row in table], axis=0) for k in range(half)]
        return [row[k] for k in range(half) for row in table]

    parts_out = [with_mates(own_out)]
    fresh_par = at_ends(lax.dynamic_index_in_dim(grad_new, jnp.where(place == 0, 1, 0), keepdims=False))
    g_par = partner(grad_now[:, 0])
    bounds = jnp.concatenate([bound_now.reshape(-1), bound_new.reshape(-1)])

    d = grad_now.shape[-1]
    own, par = {}, {}
    ga, gv, gi = {}, {}, {}
    probs, mine, came = [None] * 2, [None] * 2, [None] * 2
    for r in range(2):
        own[r, 0], par[r, 0] = [piece(grad_now, r, 0)], [piece(g_par, r)]

    def run_front(r, deps=()):
        probs[r], mine[r], send = front(
            r, per, heads, sections, meta, bounds, queries_saved, keys_saved, values, deps
        )
        came[r] = jnp.stack([partner(send[t]) for t in range(2)])

    def run_ahead(r, t, deps=()):
        here, send = ahead(r, t, heads // len(parts_out[r]), meta, own[r, t], par[r, t], parts_out[r], deps)
        if (r, t) == (1, 1):
            step = send.shape[0] // 2
            ga[r, t] = (here, jnp.concatenate([partner(send[:step]), partner(send[step:])], axis=0))
        else:
            ga[r, t] = (here, partner(send))

    def run_middle(r, t, deps=()):
        gv[r, t], gi[r, t], *joined = middle(
            r, t, meta, own[r, t], probs[r], *ga[r, t], w_value, int((r, t) == (0, 0)), deps
        )
        return joined

    def run_relay(r):
        x = joined[0] if r == 0 else gi[1, 0]
        got = [relayed(x, r, k) for k in (0, half)]
        block = pl.BlockSpec((x.shape[0], d), lambda i, *s: (0, 0))
        own[r, 1] = [(got[0], block), piece(grad_new, r)]
        par[r, 1] = [(got[1], block), piece(fresh_par)]
        return got

    def run_outer(r, deps=()):
        gs = own[r, 0] + par[r, 0] + own[r, 1] + par[r, 1]
        away = [outer(r, k, rows, meta, mine[r], came[r], gs, BF, deps) for k in range(1, half)]
        total = outer(r, 0, rows, meta, mine[r], came[r], gs, F32, [*deps, *away])
        return summed(away, total)

    run_ahead(0, 0)
    w_value, values = values_of(meta, inputs_saved, parts_value, [ga[0, 0][0], fresh_par])
    run_front(0)
    run_front(1, [probs[0]])
    joined = run_middle(0, 0, [probs[1]])
    mirror_out = hold(mirror_out, [came[0], came[1], gi[0, 0]])
    parts_out.append(with_mates(mirror_out))
    run_ahead(1, 0)
    run_middle(1, 0)
    run_relay(1)
    total1 = run_outer(1, run_relay(0))
    send_out = total1.astype(BF)
    back_out = mirrored(send_out)
    run_ahead(1, 1, [send_out])
    run_ahead(0, 1, [ga[1, 1][0]])
    run_middle(1, 1, [ga[0, 1][0]])
    run_middle(0, 1, [gi[1, 1]])
    gvs = [gv[r, t] for r in range(2) for t in range(2)]
    total, *sent = value_grads(meta, lanes, inputs_saved, gvs)
    gas = [[*ga[r, 0], *ga[r, 1]] for r in range(2)]
    total0 = run_outer(0, [total])
    out = back(1, per, heads, meta, queries_saved, keys_saved, values, probs[1], gas[1], deps=[total0])
    total = [summed([part[r] for part in sent], total[r]) for r in range(2)]
    back_value = mirrored(total[1].astype(BF))
    grad_queries, grad_keys = back(
        0, per, heads, meta, queries_saved, keys_saved, values, probs[0], gas[0], out
    )
    grad_inputs = jnp.stack([jnp.stack([gi[r, t] for t in range(2)]) for r in range(2)])[:, :, None]
    out_moment_new, out_weight_new, updated = update(
        lanes, meta, total0, back_out, out_moment, out_weight, [grad_keys]
    )
    back_value = hold(back_value, [updated])
    mean_value = (total[0] + back_value.astype(F32)) / lanes
    value_moment_new = decay_rate * value_moment + mean_value[None]
    value_weight_new = value_weight - learn_rate * value_moment_new
    return (
        grad_inputs,
        grad_queries,
        grad_keys,
        value_weight_new,
        out_weight_new,
        value_moment_new,
        out_moment_new,
    )


def solution(mesh):
    saved = P(None, None, "section", "lane", None)
    weight = P("section", "lane", None)
    return jax.shard_map(
        shards,
        mesh=mesh,
        in_specs=(
            weight,
            weight,
            weight,
            weight,
            saved,
            saved,
            saved,
            P(None, "section", "lane", None),
            P(None, "lane", None),
            P(None, None, "lane"),
            P(None, "lane"),
        ),
        out_specs=(saved, saved, saved, weight, weight, weight, weight),
        check_vma=False,
    )
```

```python
import functools
import math

import jax
import jax.numpy as jnp
from jax import lax
from jax.experimental import pallas as pl
from jax.experimental.pallas import tpu as pltpu
from jax.sharding import PartitionSpec as P

HEAD = 128
KV_HEADS = 2

decay_rate = 0.9
learn_rate = 0.01

BF = jnp.bfloat16
F32 = jnp.float32
SCALE = 1.0 / math.sqrt(HEAD)


def mm(a, b, ca, cb):
    return lax.dot_general(a, b, (((ca,), (cb,)), ((), ())), preferred_element_type=F32)


def piece(array, *lead):
    rest = array.shape[len(lead) :]
    return array, pl.BlockSpec((None,) * len(lead) + rest, lambda i, *s: lead + (0,) * len(rest))


def whole_out(shape):
    return pl.BlockSpec(shape, lambda i, *s: (0,) * len(shape))


def call(kernel, name, scalars, operands, shapes, steps=1, outs=None, scratch=(), aliases=None, deps=()):
    count = len(scalars) + len(operands)

    def body(*refs):
        kernel(*refs[:count], *refs[count + len(deps) :])

    operands = list(operands) + [(a, pl.BlockSpec(memory_space=pl.ANY)) for a in deps]
    arrays, specs = zip(*operands)
    grid = pltpu.PrefetchScalarGridSpec(
        num_scalar_prefetch=len(scalars),
        grid=(steps,),
        in_specs=list(specs),
        out_specs=outs or [whole_out(s.shape) for s in shapes],
        scratch_shapes=scratch,
    )
    aliases = {len(scalars) + i: o for i, o in (aliases or {}).items()}
    return pl.pallas_call(
        body,
        grid_spec=grid,
        out_shape=shapes,
        input_output_aliases=aliases,
        compiler_params=pltpu.CompilerParams(vmem_limit_bytes=20 * 1024 * 1024),
        cost_estimate=pl.CostEstimate(flops=1, bytes_accessed=1, transcendentals=0),
        name=name,
    )(*scalars, *arrays)


def sds(shape, dtype=BF):
    return jax.ShapeDtypeStruct(shape, dtype)


def head_start(meta, i, per):
    place = jnp.bitwise_xor(meta[1], i // per) * per + i % per
    return place * HEAD


def columns(ref, start, size):
    return ref[:, pl.ds(pl.multiple_of(start, HEAD), size)]


def hold_kernel(x, out):
    pass


def hold(x, deps):
    anywhere = pl.BlockSpec(memory_space=pl.ANY)
    shape = [sds(x.shape, x.dtype)]
    return call(hold_kernel, "hold", [], [(x, anywhere)], shape, outs=[anywhere], aliases={0: 0}, deps=deps)[0]


def cast_kernel(x, out):
    out[...] = x[...].astype(BF)


def lowered(i, rows, x, deps=()):
    d = x.shape[2]
    block = pl.BlockSpec((None, rows, d), lambda _: (0, i, 0))
    return call(cast_kernel, "lowered", [], [(x, block)], [sds((rows, d))], deps=deps)[0]


def value_kernel(lanes, meta, x, *refs):
    parts, (full, out) = refs[:-2], refs[-2:]
    rows = parts[0].shape[0]
    for r in range(2):
        for k in range(lanes):
            at = jnp.bitwise_xor(meta[3], k) * rows
            full[r, pl.ds(pl.multiple_of(at, rows), rows), :] = parts[r * lanes + k][...]
        for t in range(x.shape[1]):
            out[r, t] = mm(x[r, t, 0], full[r], 1, 0).astype(BF)


def values_of(meta, inputs, parts, deps=()):
    ticks, tok, d = inputs.shape[1], inputs.shape[3], inputs.shape[4]
    kvw = parts[0].shape[1]
    return call(
        functools.partial(value_kernel, len(parts) // 2),
        "values",
        [meta],
        [piece(inputs)] + [piece(p) for p in parts],
        [sds((2, d, kvw)), sds((2, ticks, tok, kvw))],
        deps=deps,
    )


def queries_of(half, heads, per, meta, q):
    base = half * heads * HEAD
    return jnp.concatenate([columns(q, base + head_start(meta, i, per), HEAD) for i in range(heads)], axis=0)


def front_kernel(r, per, heads, sections, meta, bounds, q, k, v, probs, mine, send):
    t = pl.program_id(0)
    tok = q.shape[0]
    place = meta[2]
    near = jnp.clip(place + t * (1 - 2 * r), 0, sections - 1)
    at = jnp.where((t == 1) & (meta[4 + r] == 1), 2 * sections + r, r * sections + near)
    bound = bounds[at]
    key_at = lax.broadcasted_iota(jnp.int32, (tok, tok), 0)
    query_at = lax.broadcasted_iota(jnp.int32, (tok, tok), 1)
    seen = (key_at <= query_at) & ((query_at >= bound) == (key_at >= bound))
    seen = jnp.concatenate([seen.astype(F32)] * heads, axis=1) > 0.5
    for s in range(2):
        half = meta[0] if s == 0 else 1 - meta[0]
        out = mine if s == 0 else send
        key, val = columns(k, half * HEAD, HEAD), columns(v, half * HEAD, HEAD)
        x = jnp.where(seen, mm(key, queries_of(half, heads, per, meta, q), 1, 1) * SCALE, -1e30)
        e = jnp.exp(x - jnp.max(x, axis=0, keepdims=True))
        p = (e * (1.0 / jnp.sum(e, axis=0, keepdims=True))).astype(BF)
        probs[s] = p
        for i in range(heads):
            out[:, i * HEAD : (i + 1) * HEAD] = mm(p[:, i * tok : (i + 1) * tok], val, 0, 0).astype(BF)


def front(r, per, heads, sections, meta, bounds, queries, keys, values, deps=()):
    ticks, tok = queries.shape[1], queries.shape[3]
    width = heads * HEAD
    operands = [
        (queries, pl.BlockSpec((None, None, None, tok, 2 * width), lambda t, *s: (r, t, 0, 0, 0))),
        (keys, pl.BlockSpec((None, None, None, tok, 2 * HEAD), lambda t, *s: (r, t, 0, 0, 0))),
        (values, pl.BlockSpec((None, None, tok, 2 * HEAD), lambda t, *s: (r, t, 0, 0))),
    ]
    outs = [
        pl.BlockSpec((None, 2, tok, heads * tok), lambda t, *s: (t, 0, 0, 0)),
        pl.BlockSpec((None, tok, width), lambda t, *s: (t, 0, 0)),
        pl.BlockSpec((None, tok, width), lambda t, *s: (t, 0, 0)),
    ]
    shapes = [sds((ticks, 2, tok, heads * tok)), sds((ticks, tok, width)), sds((ticks, tok, width))]
    return call(
        functools.partial(front_kernel, r, per, heads, sections),
        "front",
        [meta, bounds],
        operands,
        shapes,
        ticks,
        outs,
        deps=deps,
    )


def chosen(meta, r, refs):
    return refs[0][...] if len(refs) == 1 else jnp.where(meta[4 + r] == 1, refs[1][...], refs[0][...])


def ahead_kernel(r, t, parts, per, meta, *refs):
    own, par, weights = refs[: t + 1], refs[t + 1 : 2 * t + 2], refs[2 * t + 2 : -2]
    tok = own[0].shape[0]
    g = jnp.concatenate([chosen(meta, r, own), chosen(meta, r, par)], axis=0)
    for k in range(parts):
        ga = mm(g, weights[k][...], 1, 1).astype(BF)
        for j in range(per):
            for s in range(2):
                at = (k * per + j) * tok
                refs[s - 2][at : at + tok, :] = ga[s * tok : (s + 1) * tok, j * HEAD : (j + 1) * HEAD]


def ahead(r, t, per, meta, own, par, weights, deps=()):
    tok, d = own[0][1].block_shape[-2:]
    shape = (len(weights) * per * tok, HEAD)
    return call(
        functools.partial(ahead_kernel, r, t, len(weights), per),
        "ahead",
        [meta],
        own + par + [piece(w) for w in weights],
        [sds(shape)] * 2,
        deps=deps,
    )


def middle_kernel(r, t, meta, *refs):
    own = refs[: t + 1]
    probs, mine, came, w, gv_out, gi_out, *joined = refs[t + 1 :]
    h = meta[0] == 0
    a = mm(probs[0], mine[...], 1, 0).astype(BF)
    b = mm(probs[1], came[...], 1, 0).astype(BF)
    gv = jnp.concatenate([jnp.where(h, a, b), jnp.where(h, b, a)], axis=1)
    gv_out[...] = gv
    gi = (chosen(meta, r, own).astype(F32) + mm(gv, w[...], 1, 1)).astype(BF)
    gi_out[...] = gi
    if joined:
        joined[0][:, : gi.shape[1]] = gi
        joined[0][:, gi.shape[1] :] = gv


def middle(r, t, meta, own, probs, mine, came, w_value, joined, deps=()):
    tok, d = own[0][1].block_shape[-2:]
    return call(
        functools.partial(middle_kernel, r, t),
        "middle",
        [meta],
        own + [piece(probs, t), piece(mine), piece(came), piece(w_value, r)],
        [sds((tok, 2 * HEAD)), sds((tok, d))] + [sds((tok, d + 2 * HEAD))] * joined,
        deps=deps,
    )


def back_kernel(per, heads, filled, meta, q, k, v, probs, mine0, came0, mine1, came1, *refs):
    gq, gk = refs[2:] if filled else refs
    tok = q.shape[2]
    width = heads * HEAD
    for t, pair in enumerate(((mine0, came0), (mine1, came1))):
        for s in range(2):
            half = meta[0] if s == 0 else 1 - meta[0]
            base = half * width
            key, val = columns(k.at[t, 0], half * HEAD, HEAD), columns(v.at[t], half * HEAD, HEAD)
            gp = mm(val, pair[s][...], 1, 1)
            p = probs[t, s].astype(F32)
            delta = jnp.sum(p * gp, axis=0, keepdims=True)
            gs = (p * ((gp - delta) * SCALE)).astype(BF)
            for i in range(heads):
                at = pl.multiple_of(base + head_start(meta, i, per), HEAD)
                out = mm(gs[:, i * tok : (i + 1) * tok], key, 0, 0).astype(BF)
                gq.at[t, 0][:, pl.ds(at, HEAD)] = out
            out = mm(gs, queries_of(half, heads, per, meta, q.at[t, 0]), 1, 0).astype(BF)
            gk.at[t, 0][:, pl.ds(pl.multiple_of(half * HEAD, HEAD), HEAD)] = out


def back(r, per, heads, meta, queries, keys, values, probs, gas, filled=(), deps=()):
    arrays = (queries, keys)
    specs = [pl.BlockSpec((None,) + a.shape[1:], lambda i, m: (r, 0, 0, 0, 0)) for a in arrays]
    operands = list(zip(arrays, specs)) + [piece(values, r), piece(probs)] + [piece(a) for a in gas]
    operands += [(a, pl.BlockSpec(memory_space=pl.ANY)) for a in filled]
    first = len(operands) - 2
    return call(
        functools.partial(back_kernel, per, heads, bool(filled)),
        "back",
        [meta],
        operands,
        [sds(a.shape) for a in arrays],
        outs=specs,
        aliases={first: 0, first + 1: 1} if filled else {},
        deps=deps,
    )


def outer_kernel(r, meta, mine, came, *refs):
    out = refs[-1]
    total = mm(mine[0], refs[0][...], 0, 0)
    total = total + mm(came[0], refs[1][...], 0, 0)
    total = total + mm(mine[1], chosen(meta, r, refs[2:4]), 0, 0)
    total = total + mm(came[1], chosen(meta, r, refs[4:6]), 0, 0)
    out[...] = total.astype(out.dtype)


def outer(r, k, rows, meta, mine, came, gs, dtype, deps=()):
    ticks, tok = mine.shape[0], mine.shape[1]
    d = gs[0][1].block_shape[-1]
    step = min(rows, 256)
    first = k * (rows // step)
    block = pl.BlockSpec((ticks, tok, step), lambda i, m: (0, 0, first + i))
    outs = [pl.BlockSpec((step, d), lambda i, m: (i, 0))]
    return call(
        functools.partial(outer_kernel, r),
        "outer",
        [meta],
        [(mine, block), (came, block)] + gs,
        [sds((rows, d), dtype)],
        rows // step,
        outs,
        deps=deps,
    )[0]


def update_kernel(lanes, meta, own, back, moment, weight, moment_out, weight_out, done):
    grad = (own[...] + back[...].astype(F32)) / lanes
    new = decay_rate * moment[...] + grad
    moment_out[...] = new
    weight_out[...] = weight[...] - learn_rate * new
    done[...] = new[:8, :HEAD]


def update(lanes, meta, own, back, moment, weight, deps=()):
    rows, d = own.shape
    step = min(rows, 128)
    flat = pl.BlockSpec((step, d), lambda i, m: (i, 0))
    deep = pl.BlockSpec((None, step, d), lambda i, m: (0, i, 0))
    return call(
        functools.partial(update_kernel, lanes),
        "update",
        [meta],
        [(own, flat), (back, flat), (moment, deep), (weight, deep)],
        [sds(moment.shape, F32)] * 2 + [sds((8, HEAD), F32)],
        rows // step,
        [deep, deep, pl.BlockSpec((8, HEAD), lambda i, m: (0, 0))],
        deps=deps,
    )


def value_grad_kernel(meta, x, gv00, gv01, gv10, gv11, own, *refs):
    sent, total = refs[:-1], refs[-1]
    rows = own.shape[1]
    for r, gvs in enumerate(((gv00, gv01), (gv10, gv11))):
        total[...] = mm(x[r, 0, 0], gvs[0][...], 0, 0) + mm(x[r, 1, 0], gvs[1][...], 0, 0)
        for k, out in enumerate((own, *sent)):
            at = jnp.bitwise_xor(meta[3], k) * rows
            out[r] = total[pl.ds(pl.multiple_of(at, rows), rows), :].astype(out.dtype)


def value_grads(meta, lanes, inputs, gvs, deps=()):
    d = inputs.shape[4]
    kvw = KV_HEADS * HEAD
    rows = d // lanes
    shapes = [sds((2, rows, kvw), F32)] + [sds((2, rows, kvw))] * (lanes - 1)
    return call(
        value_grad_kernel,
        "value_grads",
        [meta],
        [piece(a) for a in (inputs, *gvs)],
        shapes,
        scratch=[pltpu.VMEM((d, kvw), F32)],
        deps=deps,
    )


def shards(
    value_weight,
    out_weight,
    value_moment,
    out_moment,
    inputs_saved,
    queries_saved,
    keys_saved,
    grad_now,
    grad_new,
    bound_now,
    bound_new,
):
    sections = lax.axis_size("section")
    lanes = lax.axis_size("lane")
    place = lax.axis_index("section")
    lane = lax.axis_index("lane")
    half = lanes // KV_HEADS
    h, c = lane // half, lane % half
    rows = out_weight.shape[1]
    per = rows // HEAD
    heads = per * half
    at_end = (place == sections - 1, place == 0)
    meta = jnp.stack([h, c, place, lane, *at_end]).astype(jnp.int32)

    def at_lane(x, k):
        return lax.ppermute(x, "lane", [(i, i ^ k) for i in range(lanes)])

    def partner(x):
        return at_lane(x, half)

    def mirrored(x):
        return lax.ppermute(x, "section", [(i, sections - 1 - i) for i in range(sections)])

    def relayed(x, r, k=0):
        by = 1 if r else -1
        pairs = [
            (i * lanes + j, (i + by) * lanes + (j ^ k))
            for i in range(sections)
            for j in range(lanes)
            if 0 <= i + by < sections
        ]
        return lax.ppermute(x, ("section", "lane"), pairs)

    def at_ends(x):
        pairs = [(i * lanes + j, i * lanes + (j ^ half)) for i in (0, sections - 1) for j in range(lanes)]
        return lax.ppermute(x, ("section", "lane"), pairs)

    def spread(x, count):
        return [x] + [at_lane(x, k) for k in range(1, count)]

    def summed(away, total):
        for k, part in enumerate(away):
            if part.shape[0] == rows:
                step = part.shape[0] // 4
                pieces = [at_lane(part[i : i + step], k + 1) for i in range(0, part.shape[0], step)]
                part = jnp.concatenate(pieces, axis=0)
            else:
                part = at_lane(part, k + 1)
            total = total + part.astype(F32)
        return total

    own_value = value_weight[0].astype(BF)
    mirror_value = mirrored(own_value)
    own_out = lowered(0, rows, out_weight)
    mirror_out = mirrored(hold(own_out, [mirror_value]))
    parts_value = spread(own_value, lanes) + spread(mirror_value, lanes)
    cut = rows // 4

    def with_mates(x):
        pieces = [x[i : i + cut] for i in range(0, rows, cut)]
        table = [spread(p, half) for p in pieces]
        if cut % HEAD:
            return [jnp.concatenate([row[k] for row in table], axis=0) for k in range(half)]
        return [row[k] for k in range(half) for row in table]

    parts_out = [with_mates(own_out)]
    fresh_par = at_ends(lax.dynamic_index_in_dim(grad_new, jnp.where(place == 0, 1, 0), keepdims=False))
    g_par = partner(grad_now[:, 0])
    bounds = jnp.concatenate([bound_now.reshape(-1), bound_new.reshape(-1)])

    d = grad_now.shape[-1]
    own, par = {}, {}
    ga, gv, gi = {}, {}, {}
    probs, mine, came = [None] * 2, [None] * 2, [None] * 2
    for r in range(2):
        own[r, 0], par[r, 0] = [piece(grad_now, r, 0)], [piece(g_par, r)]

    def run_front(r, deps=()):
        probs[r], mine[r], send = front(
            r, per, heads, sections, meta, bounds, queries_saved, keys_saved, values, deps
        )
        came[r] = jnp.stack([partner(send[t]) for t in range(2)])

    def run_ahead(r, t, deps=()):
        here, send = ahead(r, t, heads // len(parts_out[r]), meta, own[r, t], par[r, t], parts_out[r], deps)
        if (r, t) == (1, 1):
            step = send.shape[0] // 2
            ga[r, t] = (here, jnp.concatenate([partner(send[:step]), partner(send[step:])], axis=0))
        else:
            ga[r, t] = (here, partner(send))

    def run_middle(r, t, deps=()):
        gv[r, t], gi[r, t], *joined = middle(
            r, t, meta, own[r, t], probs[r], *ga[r, t], w_value, int((r, t) == (0, 0)), deps
        )
        return joined

    def run_relay(r):
        x = joined[0] if r == 0 else gi[1, 0]
        got = relayed(x, r)
        far = partner(got[:, :d]) if r == 0 else relayed(x, r, half)
        own[r, 1] = [(got, pl.BlockSpec((x.shape[0], d), lambda i, *s: (0, 0))), piece(grad_new, r)]
        par[r, 1] = [piece(far), piece(fresh_par)]
        return [got]

    def run_outer(r, deps=()):
        gs = own[r, 0] + par[r, 0] + own[r, 1] + par[r, 1]
        away = [outer(r, k, rows, meta, mine[r], came[r], gs, BF, deps) for k in range(1, half)]
        total = outer(r, 0, rows, meta, mine[r], came[r], gs, F32, [*deps, *away])
        return summed(away, total)

    run_ahead(0, 0)
    w_value, values = values_of(meta, inputs_saved, parts_value, [ga[0, 0][0], fresh_par])
    run_front(0)
    run_front(1, [probs[0]])
    joined = run_middle(0, 0, [probs[1]])
    mirror_out = hold(mirror_out, [came[0], came[1]])
    parts_out.append(with_mates(mirror_out))
    run_ahead(1, 0)
    run_middle(1, 0)
    run_relay(1)
    total1 = run_outer(1, run_relay(0))
    send_out = total1.astype(BF)
    back_out = mirrored(send_out)
    run_ahead(1, 1, [send_out])
    run_ahead(0, 1, [ga[1, 1][0]])
    run_middle(1, 1, [ga[0, 1][0]])
    run_middle(0, 1, [gi[1, 1]])
    gvs = [gv[r, t] for r in range(2) for t in range(2)]
    total, *sent = value_grads(meta, lanes, inputs_saved, gvs)
    gas = [[*ga[r, 0], *ga[r, 1]] for r in range(2)]
    total0 = run_outer(0, [total])
    out = back(1, per, heads, meta, queries_saved, keys_saved, values, probs[1], gas[1], deps=[total0])
    total = [summed([part[r] for part in sent], total[r]) for r in range(2)]
    back_value = mirrored(total[1].astype(BF))
    grad_queries, grad_keys = back(
        0, per, heads, meta, queries_saved, keys_saved, values, probs[0], gas[0], out
    )
    grad_inputs = jnp.stack([jnp.stack([gi[r, t] for t in range(2)]) for r in range(2)])[:, :, None]
    out_moment_new, out_weight_new, updated = update(
        lanes, meta, total0, back_out, out_moment, out_weight, [grad_keys]
    )
    back_value = hold(back_value, [updated])
    mean_value = (total[0] + back_value.astype(F32)) / lanes
    value_moment_new = decay_rate * value_moment + mean_value[None]
    value_weight_new = value_weight - learn_rate * value_moment_new
    return (
        grad_inputs,
        grad_queries,
        grad_keys,
        value_weight_new,
        out_weight_new,
        value_moment_new,
        out_moment_new,
    )


def solution(mesh):
    saved = P(None, None, "section", "lane", None)
    weight = P("section", "lane", None)
    return jax.shard_map(
        shards,
        mesh=mesh,
        in_specs=(
            weight,
            weight,
            weight,
            weight,
            saved,
            saved,
            saved,
            P(None, "section", "lane", None),
            P(None, "lane", None),
            P(None, None, "lane"),
            P(None, "lane"),
        ),
        out_specs=(saved, saved, saved, weight, weight, weight, weight),
        check_vma=False,
    )
```
